256 devices in a mesh: inner: 16 (over x, z_lo, core), outer: 16 (over y, z_hi).
Axes of the slice: x: 4, y: 4, z: 8 (z_hi: 4, z_lo: 2; z = z_hi * 2 + z_lo), core: 2. Of those that a mesh axis runs over, the one named last changes fastest.
Arguments:
- queries: bfloat16 [65536, 3072], P(('inner', 'outer')), may hold values from -30 to 30
- keys: bfloat16 [65536, 3072], P(('inner', 'outer')), may hold values from -30 to 30
- values: bfloat16 [65536, 3072], P(('inner', 'outer')), may hold values from -6 to 6
- frame_mask: int32 [512, 30], P(('inner', 'outer')), may hold values from 0 to 1, as said below
- query_order: int32 [512], P(('inner', 'outer')), may hold values from 0 to 511, as said below
Outputs:
- attended: bfloat16 [65536, 3072], P(('inner', 'outer'))
The draws below stay inside these ranges and needn't reach their ends.
Inputs may be any that keep to these rules, and one draw needn't show every extreme that they name: query_order[b] // 2 == b // 2: each device's blocks take that device's mask rows in some order. `frame_mask`: entries naming a device outside the clip are 0; for each row r, the entry at offsets 0 and slot r % 2 is 1, so every query block has at least one live key block on its own device.
All inputs are finite; a program needn't handle non-finite values.
Results may differ from the reference program's by a relative error of at most 0.0056.
Values may be sent and summed in bfloat16 or wider, within the bound.
A program may use at most 128 MiB of HBM per device.

```python
import jax
import jax.numpy as jnp
from jax import lax

HEADS = 24
D = 3072
TOK_DEV = 256
BPD = 2
WINDOW = 30
TOKENS = 65536
BLOCKS = 512
N_INNER = 16
N_OUTER = 16
DEVICES = 256


def draw_queries(key, part):
    key = jax.random.fold_in(key, 11)
    fresh = jnp.clip(jax.random.normal(key, (TOKENS, D), jnp.float32), -6.0, 6.0)
    return fresh.astype(jnp.bfloat16)


def draw_keys(key, part):
    key = jax.random.fold_in(key, 12)
    fresh = jnp.clip(jax.random.normal(key, (TOKENS, D), jnp.float32), -6.0, 6.0)
    return fresh.astype(jnp.bfloat16)


def draw_frame_mask(key, part):
    key = jax.random.fold_in(key, 21)
    first, second = jax.random.split(key)
    level = jax.random.randint(first, (BLOCKS, 1), 3, 9)
    coin = jax.random.randint(second, (BLOCKS, WINDOW), 0, 8)
    rows = jnp.arange(BLOCKS, dtype=jnp.int32)[:, None]
    cols = jnp.arange(WINDOW, dtype=jnp.int32)[None, :]
    device = rows // BPD
    frame = device // N_OUTER
    place = device % N_OUTER
    step = cols // (3 * BPD) - 2
    side = cols // BPD % 3 - 1
    slot = cols % BPD
    inside = (frame + step >= 0) & (frame + step < N_INNER) & (place + side >= 0) & (place + side < N_OUTER)
    own = (step == 0) & (side == 0) & (slot == rows % BPD)
    live = (coin < level - jnp.abs(step)) & inside | own
    return live.astype(jnp.int32)


def draw_query_order(key, part):
    key = jax.random.fold_in(key, 31)
    keyset = jax.random.split(key, DEVICES)
    perms = jax.vmap(lambda one: jax.random.permutation(one, BPD))(keyset).astype(jnp.int32)
    offsets = BPD * jnp.arange(DEVICES, dtype=jnp.int32)[:, None]
    return (perms + offsets).reshape(-1).astype(jnp.int32)


def block_scale(stream_key, extent, shards, least, top_value):
    def one(position, blocks):
        steps = jax.random.uniform(jax.random.fold_in(jax.random.fold_in(stream_key, 6), position), (blocks,), jnp.float32, least / len(shards), top_value / len(shards))
        return jnp.repeat(jnp.exp(steps), extent[position] // blocks).reshape((-1,) + (1,) * (len(extent) - position - 1))

    level = one(*shards[0])
    for cut in shards[1:]:
        level = level * one(*cut)
    return level


def gaussian(key, extent, spread, limit, shards=(), kind=jnp.bfloat16):
    values = jax.random.normal(key, extent, jnp.float32) * spread
    if len(shards) > 0:
        values = block_scale(key, extent, shards, -0.22, 0.18) * values
    return jnp.clip(values, min=-limit, max=limit).astype(kind)


def setup_inputs(seed: int = 0) -> dict:
    arg_keys = jax.random.split(jax.random.key(seed), 6)
    return {
        "queries": draw_queries(jax.random.fold_in(arg_keys[5], 71), 0),
        "keys": draw_keys(jax.random.fold_in(arg_keys[5], 71), 0),
        "values": gaussian(arg_keys[2], (TOKENS, D), 1.0, 6.0, ((0, 256),)),
        "frame_mask": draw_frame_mask(jax.random.fold_in(arg_keys[5], 71), 0),
        "query_order": draw_query_order(jax.random.fold_in(arg_keys[5], 71), 0),
    }


def attend(qrows, live, window):
    tok = qrows.shape[0]
    dim = qrows.shape[1]
    size = dim // HEADS
    blocks = live.shape[0]
    grid = jnp.repeat(jnp.repeat(live.reshape(blocks, -1) > 0, tok // blocks, axis=0), tok // blocks, axis=1)
    query = qrows.astype(jnp.float32).reshape(tok, HEADS, size)
    keyset = window[0].astype(jnp.float32).reshape(-1, HEADS, size)
    valset = window[1].astype(jnp.float32).reshape(-1, HEADS, size)
    score = jnp.einsum('qhd,khd->hqk', query, keyset) * (size ** -0.5)
    top = jnp.max(jnp.where(grid[None], score, -1e30), axis=-1)
    prob = jnp.exp(jnp.where(grid[None], score - top[..., None], -1e30))
    total = jnp.sum(prob, axis=-1)
    rounded = prob.astype(jnp.bfloat16).astype(jnp.float32)
    numer = jnp.einsum('hqk,khd->qhd', rounded, valset)
    partial_out = (numer / jnp.maximum(total.T, 1.0)[..., None]).reshape(tok, dim).astype(jnp.bfloat16)
    return partial_out, top.T, total.T


def combine(parts):
    tops = jnp.stack([p[1] for p in parts])
    totals = jnp.stack([p[2] for p in parts])
    partial_set = jnp.stack([p[0] for p in parts]).astype(jnp.float32)
    tok = partial_set.shape[1]
    dim = partial_set.shape[2]
    best = jnp.max(tops, axis=0)
    weight = jnp.exp(tops - best[None]) * totals
    denom = jnp.sum(weight, axis=0)
    numer = jnp.sum(weight[..., None] * partial_set.reshape(3, tok, HEADS, dim // HEADS), axis=0)
    return (numer / denom[..., None]).reshape(tok, dim).astype(jnp.bfloat16)


def reference(queries, keys, values, frame_mask, query_order):
    count_in = N_INNER
    count_out = N_OUTER
    stacked = jnp.stack([keys, values]).reshape(2, count_in, count_out, TOK_DEV, D)
    stacked = jnp.pad(stacked, ((0, 0), (2, 2), (1, 1), (0, 0), (0, 0)))
    query_sets = queries.reshape(count_in * count_out, TOK_DEV, D)
    rows_all = frame_mask[query_order].reshape(count_in * count_out, BPD, 5, 3, BPD)
    zero = jnp.zeros((), jnp.int32)

    def one(index):
        frame = (index // count_out).astype(jnp.int32)
        place = (index % count_out).astype(jnp.int32)
        window = lax.dynamic_slice(stacked, (zero, frame, place, zero, zero), (2, 5, 3, TOK_DEV, D))
        live = rows_all[index]
        parts = [attend(query_sets[index], live[:, :, side, :], window[:, :, side].reshape(2, 5 * TOK_DEV, D)) for side in range(3)]
        return combine(parts)

    result = lax.map(one, jnp.arange(count_in * count_out, dtype=jnp.int32))
    return result.reshape(TOKENS, D)
```

```python
import math

import jax
import jax.numpy as jnp
from jax import lax
from jax.experimental import pallas as pl
from jax.experimental.pallas import tpu as pltpu
from jax.sharding import PartitionSpec as P

HEADS = 24
SIZE = 128
RING = 8
PER = HEADS // RING
TOK = 256
MESH = pl.DeviceIdType.MESH
DEAD = -1e30
EXPONENT = math.log2(math.e) / math.sqrt(SIZE)


def body(order_ref, mask_ref, q_ref, k_ref, v_ref, out_ref,
         qbuf, kv, obuf, mine, marks, bias, score,
         q_send, q_recv, y_send, y_recv, f_send, f_recv, m_send, m_recv, o_send, o_recv):
    inner = lax.axis_index("inner")
    outer = lax.axis_index("outer")
    x, lo, core = inner // 4, (inner // 2) % 2, inner % 2
    y, hi = outer // 4, outer % 4
    z = 2 * hi + lo
    home = lo == core

    def device(x_at, y_at, z_at, core_at):
        return (x_at * 4 + (z_at % 2) * 2 + core_at, y_at * 4 + z_at // 2)

    def owner(place, parity):
        return device(x, y, 2 * place + core, parity)

    up = device(x, (y + 1) % 4, z, core)
    down = device(x, (y + 3) % 4, z, core)
    after = device((x + core) % 4, y, z, 1 - core)
    before = device((x + 3 + core) % 4, y, z, 1 - core)

    barrier = pltpu.get_barrier_semaphore()
    for peer in (up, down, after, before):
        pl.semaphore_signal(barrier, inc=1, device_id=peer, device_id_type=MESH)
    for d in range(1, RING):
        pl.semaphore_signal(
            barrier, inc=1, device_id=device(x, y, (z + d) % RING, lo), device_id_type=MESH
        )

    @pl.when(jnp.logical_not(home))
    def _():
        pl.semaphore_signal(barrier, inc=1, device_id=device(x, y, z, lo), device_id_type=MESH)

    for place in range(4):
        for parity in range(2):
            @pl.when(jnp.logical_not(home & (place == hi) & (parity == core)))
            def _():
                pl.semaphore_signal(
                    barrier, inc=1, device_id=owner(place, parity), device_id_type=MESH
                )

    mine[...] = jnp.zeros_like(mine)
    for row in range(2):
        picked = order_ref[row] - 2 * (inner * 16 + outer)
        live = jnp.where(picked == 0, mask_ref[0:1, :], mask_ref[1:2, :])
        mine[row : row + 1, 0:30] = jnp.where(live > 0, 0.0, DEAD)

    pl.semaphore_wait(barrier, 20 - 2 * home.astype(jnp.int32))

    slot = 2 * hi + core

    def move(source, target, send, recv, to, local):
        if local is None:
            pltpu.make_async_remote_copy(
                src_ref=source, dst_ref=target, send_sem=send, recv_sem=recv,
                device_id=to, device_id_type=MESH,
            ).start()
        else:
            @pl.when(local)
            def _():
                pltpu.make_async_copy(source, target, recv).start()

            @pl.when(jnp.logical_not(local))
            def _():
                pltpu.make_async_remote_copy(
                    src_ref=source, dst_ref=target, send_sem=send, recv_sem=recv,
                    device_id=to, device_id_type=MESH,
                ).start()

    steps = (4, 3, 5, 2, 6, 1, 7, 0)
    for n, d in enumerate(steps):
        to = device(x, y, (z + d) % RING, lo)
        move(mine, marks.at[slot], m_send.at[n], m_recv.at[slot], to, home if d == 0 else None)

    def spread(h, carry):
        for t in range(3):
            for n, d in enumerate(steps):
                there = (z + d) % RING
                to = device(x, y, there, lo)
                cols = pl.ds(pl.multiple_of((there * PER + h) * SIZE, SIZE), SIZE)
                source = (k_ref, v_ref, q_ref)[t].at[:, cols]
                if t < 2:
                    target = kv.at[h, 1 + hi, 2 + core, t]
                else:
                    target = qbuf.at[h, slot]
                move(source, target, q_send.at[h, n, t], q_recv.at[h, slot, t], to,
                     home if d == 0 else None)
        return carry

    lax.fori_loop(0, PER, spread, 0)

    for s in range(RING):
        pltpu.make_async_copy(mine, marks.at[s], m_recv.at[s]).wait()

    def widen(s, carry):
        rows = marks[s]
        for w in range(30):
            bias[s, w] = jnp.broadcast_to(rows[:, w : w + 1], (8, SIZE))
        return carry

    lax.fori_loop(0, RING, widen, 0)

    def forward_copies(h, place):
        source = kv.at[h, place, pl.ds(2, 2)]
        return (
            pltpu.make_async_remote_copy(
                src_ref=source, dst_ref=kv.at[h, place, pl.ds(0, 2)],
                send_sem=f_send.at[h, place, 0], recv_sem=f_recv.at[h, place, 0],
                device_id=after, device_id_type=MESH),
            pltpu.make_async_remote_copy(
                src_ref=source, dst_ref=kv.at[h, place, pl.ds(4, 2)],
                send_sem=f_send.at[h, place, 1], recv_sem=f_recv.at[h, place, 1],
                device_id=before, device_id_type=MESH),
        )

    def edge_copy(h, side):
        return pltpu.make_async_remote_copy(
            src_ref=kv.at[h, 4 if side == 0 else 1, pl.ds(2, 2)],
            dst_ref=kv.at[h, 0 if side == 0 else 5, pl.ds(2, 2)],
            send_sem=y_send.at[h, side], recv_sem=y_recv.at[h, side],
            device_id=up if side == 0 else down, device_id_type=MESH)

    def send_out(h, j):
        place, parity = j // 2, j % 2
        cols = pl.ds(pl.multiple_of((z * PER + h) * SIZE, SIZE), SIZE)
        move(obuf.at[h, j], out_ref.at[:, cols], o_send.at[h, j], o_recv.at[h, z],
             owner(place, parity), home & (place == hi) & (parity == core))

    def attend(h, j):
        place, parity = j // 2, j % 2
        query = qbuf[h, j]
        top = jnp.full((TOK, SIZE), DEAD, jnp.float32)
        for s in range(15):
            step, side = s // 3, s % 3
            keyset = kv[h, place + side, parity + step, 0]
            raw = lax.dot_general(query, keyset, (((1,), (1,)), ((), ())),
                                  preferred_element_type=jnp.float32)
            for slot_at in range(2):
                w = 6 * step + 2 * side + slot_at
                part = raw[:, slot_at * SIZE : (slot_at + 1) * SIZE]
                upper = part[:SIZE] + bias[j, w, 0:1, :]
                lower = part[SIZE:] + bias[j, w, 1:2, :]
                part = jnp.concatenate([upper, lower], axis=0)
                score[2 * s + slot_at] = part
                top = jnp.maximum(top, part)
        top = jnp.max(top, axis=1, keepdims=True)
        total = jnp.zeros((TOK, SIZE), jnp.float32)
        numer = jnp.zeros((TOK, SIZE), jnp.float32)
        for s in range(15):
            step, side = s // 3, s % 3
            valset = kv[h, place + side, parity + step, 1]
            left = jnp.exp2((score[2 * s] - top) * EXPONENT)
            right = jnp.exp2((score[2 * s + 1] - top) * EXPONENT)
            total = total + left + right
            prob = jnp.concatenate([left, right], axis=1).astype(jnp.bfloat16)
            numer = numer + jnp.dot(prob, valset, preferred_element_type=jnp.float32)
        total = jnp.sum(total, axis=1, keepdims=True)
        obuf[h, j] = (numer / total).astype(jnp.bfloat16)

    def head(h, carry):
        for place in (3, 0, 1, 2):
            for parity in range(2):
                for t in range(2):
                    piece = kv.at[h, 1 + place, 2 + parity, t]
                    pltpu.make_async_copy(piece, piece, q_recv.at[h, 2 * place + parity, t]).wait()
            if place == 3:
                edge_copy(h, 0).start()
            if place == 0:
                edge_copy(h, 1).start()
            for copy in forward_copies(h, 1 + place):
                copy.start()
        for side in range(2):
            edge_copy(h, side).wait_recv()
            for copy in forward_copies(h, 5 * side):
                copy.start()
        for s in range(RING):
            pltpu.make_async_copy(qbuf.at[h, s], qbuf.at[h, s], q_recv.at[h, s, 2]).wait()

        @pl.when(h == PER - 1)
        def _():
            def early(n, carry):
                send_out(n // RING, n % RING)
                return carry

            lax.fori_loop(0, (PER - 1) * RING, early, 0)

        for place in range(6):
            for copy in forward_copies(h, place):
                copy.wait_recv()

        def one(j, carry):
            attend(h, j)

            @pl.when(h == PER - 1)
            def _():
                send_out(h, j)

            return carry

        lax.fori_loop(0, RING, one, 0)
        return carry

    lax.fori_loop(0, PER, head, 0)

    def finish(h, carry):
        for s in range(RING):
            cols = pl.ds(pl.multiple_of((s * PER + h) * SIZE, SIZE), SIZE)
            piece = out_ref.at[:, cols]
            pltpu.make_async_copy(piece, piece, o_recv.at[h, s]).wait()
        for n, d in enumerate(steps):
            for t in range(3):
                piece = qbuf.at[h, n]
                if d == 0:
                    @pl.when(jnp.logical_not(home))
                    def _():
                        pltpu.make_async_copy(piece, piece, q_send.at[h, n, t]).wait()
                else:
                    pltpu.make_async_copy(piece, piece, q_send.at[h, n, t]).wait()
        for side in range(2):
            edge_copy(h, side).wait_send()
        for place in range(6):
            for copy in forward_copies(h, place):
                copy.wait_send()
        for j in range(RING):
            place, parity = j // 2, j % 2

            @pl.when(jnp.logical_not(home & (place == hi) & (parity == core)))
            def _():
                piece = obuf.at[h, j]
                pltpu.make_async_copy(piece, piece, o_send.at[h, j]).wait()
        return carry

    lax.fori_loop(0, PER, finish, 0)
    for n, d in enumerate(steps):
        if d == 0:
            @pl.when(jnp.logical_not(home))
            def _():
                pltpu.make_async_copy(mine, mine, m_send.at[n]).wait()
        else:
            pltpu.make_async_copy(mine, mine, m_send.at[n]).wait()


def shards(queries, keys, values, frame_mask, query_order):
    anywhere = pl.BlockSpec(memory_space=pltpu.HBM)
    dma = pltpu.SemaphoreType.DMA
    return pl.pallas_call(
        body,
        out_shape=jax.ShapeDtypeStruct(queries.shape, queries.dtype),
        in_specs=[
            pl.BlockSpec(memory_space=pltpu.SMEM),
            pl.BlockSpec(memory_space=pltpu.VMEM),
            anywhere, anywhere, anywhere,
        ],
        out_specs=anywhere,
        scratch_shapes=[
            pltpu.VMEM((PER, RING, TOK, SIZE), jnp.bfloat16),
            pltpu.VMEM((PER, 6, 6, 2, TOK, SIZE), jnp.bfloat16),
            pltpu.VMEM((PER, RING, TOK, SIZE), jnp.bfloat16),
            pltpu.VMEM((8, SIZE), jnp.float32),
            pltpu.VMEM((RING, 8, SIZE), jnp.float32),
            pltpu.VMEM((RING, 30, 8, SIZE), jnp.float32),
            pltpu.VMEM((30, TOK, SIZE), jnp.float32),
            dma((PER, RING, 3)), dma((PER, RING, 3)),
            dma((PER, 2)), dma((PER, 2)),
            dma((PER, 6, 2)), dma((PER, 6, 2)),
            dma((RING,)), dma((RING,)),
            dma((PER, RING)), dma((PER, RING)),
        ],
        compiler_params=pltpu.CompilerParams(
            collective_id=0, has_side_effects=True, vmem_limit_bytes=48 << 20
        ),
        cost_estimate=pl.CostEstimate(
            flops=12_000_000_000, bytes_accessed=7_000_000, transcendentals=24_000_000
        ),
        name="ring_attention",
    )(query_order, frame_mask, queries, keys, values)


def solution(mesh):
    placed = (
        P(("inner", "outer"), None),
        P(("inner", "outer"), None),
        P(("inner", "outer"), None),
        P(("inner", "outer"), None),
        P(("inner", "outer")),
    )
    return jax.shard_map(
        shards, mesh=mesh, in_specs=placed, out_specs=P(("inner", "outer"), None), check_vma=False
    )
```

```python
import math

import jax
import jax.numpy as jnp
from jax import lax
from jax.experimental import pallas as pl
from jax.experimental.pallas import tpu as pltpu
from jax.sharding import PartitionSpec as P

HEADS = 24
SIZE = 128
RING = 8
PER = HEADS // RING
TOK = 256
MESH = pl.DeviceIdType.MESH
DEAD = -1e30
EXPONENT = math.log2(math.e) / math.sqrt(SIZE)


def body(order_ref, mask_ref, q_ref, k_ref, v_ref, out_ref,
         qbuf, kv, obuf, mine, marks, bias, score,
         q_send, q_recv, y_send, y_recv, f_send, f_recv, m_send, m_recv, o_send, o_recv):
    inner = lax.axis_index("inner")
    outer = lax.axis_index("outer")
    x, lo, core = inner // 4, (inner // 2) % 2, inner % 2
    y, hi = outer // 4, outer % 4
    z = 2 * hi + lo
    home = lo == core

    def device(x_at, y_at, z_at, core_at):
        return (x_at * 4 + (z_at % 2) * 2 + core_at, y_at * 4 + z_at // 2)

    def owner(place, parity):
        return device(x, y, 2 * place + core, parity)

    up = device(x, (y + 1) % 4, z, core)
    down = device(x, (y + 3) % 4, z, core)
    after = device((x + core) % 4, y, z, 1 - core)
    before = device((x + 3 + core) % 4, y, z, 1 - core)

    barrier = pltpu.get_barrier_semaphore()
    for d in range(1, RING):
        pl.semaphore_signal(
            barrier, inc=1, device_id=device(x, y, (z + d) % RING, lo), device_id_type=MESH
        )

    @pl.when(jnp.logical_not(home))
    def _():
        pl.semaphore_signal(barrier, inc=1, device_id=device(x, y, z, lo), device_id_type=MESH)

    for place in range(4):
        pl.semaphore_signal(
            barrier, inc=1, device_id=owner(place, 1 - lo), device_id_type=MESH
        )
    for peer in (up, down, device((x + 2 * core + 3) % 4, y, z, 1 - core)):
        pl.semaphore_signal(barrier, inc=1, device_id=peer, device_id_type=MESH)

    mine[...] = jnp.zeros_like(mine)
    for row in range(2):
        picked = order_ref[row] - 2 * (inner * 16 + outer)
        live = jnp.where(picked == 0, mask_ref[0:1, :], mask_ref[1:2, :])
        mine[row : row + 1, 0:30] = jnp.where(live > 0, 0.0, DEAD)

    pl.semaphore_wait(barrier, 15 - home.astype(jnp.int32))

    slot = 2 * hi + core

    def move(source, target, send, recv, to, local):
        if local is None:
            pltpu.make_async_remote_copy(
                src_ref=source, dst_ref=target, send_sem=send, recv_sem=recv,
                device_id=to, device_id_type=MESH,
            ).start()
        else:
            @pl.when(local)
            def _():
                pltpu.make_async_copy(source, target, recv).start()

            @pl.when(jnp.logical_not(local))
            def _():
                pltpu.make_async_remote_copy(
                    src_ref=source, dst_ref=target, send_sem=send, recv_sem=recv,
                    device_id=to, device_id_type=MESH,
                ).start()

    steps = (4, 3, 5, 2, 6, 1, 7, 0)
    def spread(h, t):
        for n, d in enumerate(steps):
            there = (z + d) % RING
            to = device(x, y, there, lo)
            cols = pl.ds(pl.multiple_of((there * PER + h) * SIZE, SIZE), SIZE)
            source = (k_ref, v_ref, q_ref)[t].at[:, cols]
            if t < 2:
                target = kv.at[h, 1 + hi, 2 + core, t]
            else:
                target = qbuf.at[h, slot]
            move(source, target, q_send.at[h, n, t], q_recv.at[h, slot, t], to,
                 home if d == 0 else None)

    def spread_kv(h, carry):
        spread(h, 0)
        spread(h, 1)
        return carry

    def spread_q(h, carry):
        spread(h, 2)
        return carry

    lax.fori_loop(0, PER, spread_kv, 0)
    for n, d in enumerate(steps):
        to = device(x, y, (z + d) % RING, lo)
        move(mine, marks.at[slot], m_send.at[n], m_recv.at[slot], to, home if d == 0 else None)
    lax.fori_loop(0, PER, spread_q, 0)

    def forward_copies(h, place):
        source = kv.at[h, place, pl.ds(2, 2)]
        return (
            pltpu.make_async_remote_copy(
                src_ref=source, dst_ref=kv.at[h, place, pl.ds(0, 2)],
                send_sem=f_send.at[h, place, 0], recv_sem=f_recv.at[h, place, 0],
                device_id=after, device_id_type=MESH),
            pltpu.make_async_remote_copy(
                src_ref=source, dst_ref=kv.at[h, place, pl.ds(4, 2)],
                send_sem=f_send.at[h, place, 1], recv_sem=f_recv.at[h, place, 1],
                device_id=before, device_id_type=MESH),
        )

    def edge_copy(h, side):
        return pltpu.make_async_remote_copy(
            src_ref=kv.at[h, 4 if side == 0 else 1, pl.ds(2, 2)],
            dst_ref=kv.at[h, 0 if side == 0 else 5, pl.ds(2, 2)],
            send_sem=y_send.at[h, side], recv_sem=y_recv.at[h, side],
            device_id=up if side == 0 else down, device_id_type=MESH)

    def send_out(h, j):
        place, parity = j // 2, j % 2
        cols = pl.ds(pl.multiple_of((z * PER + h) * SIZE, SIZE), SIZE)
        move(obuf.at[h, j], out_ref.at[:, cols], o_send.at[h, j], o_recv.at[h, z],
             owner(place, parity), home & (place == hi) & (parity == core))

    def attend(h, j):
        place, parity = j // 2, j % 2
        query = qbuf[h, j]
        top = jnp.full((TOK, SIZE), DEAD, jnp.float32)
        for s in range(15):
            step, side = s // 3, s % 3
            keyset = kv[h, place + side, parity + step, 0]
            raw = lax.dot_general(query, keyset, (((1,), (1,)), ((), ())),
                                  preferred_element_type=jnp.float32)
            for slot_at in range(2):
                w = 6 * step + 2 * side + slot_at
                part = raw[:, slot_at * SIZE : (slot_at + 1) * SIZE]
                upper = part[:SIZE] + bias[j, w, 0:1, :]
                lower = part[SIZE:] + bias[j, w, 1:2, :]
                part = jnp.concatenate([upper, lower], axis=0)
                score[2 * s + slot_at] = part
                top = jnp.maximum(top, part)
        top = jnp.max(top, axis=1, keepdims=True)
        total = jnp.zeros((TOK, SIZE), jnp.float32)
        numer = jnp.zeros((TOK, SIZE), jnp.float32)
        for s in range(15):
            step, side = s // 3, s % 3
            valset = kv[h, place + side, parity + step, 1]
            left = jnp.exp2((score[2 * s] - top) * EXPONENT)
            right = jnp.exp2((score[2 * s + 1] - top) * EXPONENT)
            total = total + left + right
            prob = jnp.concatenate([left, right], axis=1).astype(jnp.bfloat16)
            numer = numer + jnp.dot(prob, valset, preferred_element_type=jnp.float32)
        total = jnp.sum(total, axis=1, keepdims=True)
        obuf[h, j] = (numer / total).astype(jnp.bfloat16)

    def gather(h, carry):
        for n in range(4):
            place = (3, 0, 1, 2)[n]
            for parity in range(2):
                for t in range(2):
                    piece = kv.at[h, 1 + place, 2 + parity, t]
                    pltpu.make_async_copy(piece, piece, q_recv.at[h, 2 * place + parity, t]).wait()
            if place == 3:
                edge_copy(h, 0).start()
            if place == 0:
                edge_copy(h, 1).start()
            for copy in forward_copies(h, 1 + place):
                copy.start()
        for side in range(2):
            edge_copy(h, side).wait_recv()
            for copy in forward_copies(h, 5 * side):
                copy.start()
        return carry

    lax.fori_loop(0, PER, gather, 0)

    for s in range(RING):
        pltpu.make_async_copy(mine, marks.at[s], m_recv.at[s]).wait()

    def widen(s, carry):
        rows = marks[s]
        for w in range(30):
            bias[s, w] = jnp.broadcast_to(rows[:, w : w + 1], (2, SIZE))
        return carry

    lax.fori_loop(0, RING, widen, 0)

    def head(h, carry):
        for place in range(6):
            for copy in forward_copies(h, place):
                copy.wait_recv()

        def one(n, carry):
            rank = n // 2
            even = jnp.where(rank == 0, 4, jnp.where(rank == 1, 2, jnp.where(rank == 2, 6, 0)))
            odd = jnp.where(rank == 0, 3, jnp.where(rank == 1, 5, jnp.where(rank == 2, 1, 7)))
            away = jnp.where(home, even, odd)
            j = 2 * (((z - away + RING) % RING) // 2) + n % 2
            pltpu.make_async_copy(qbuf.at[h, j], qbuf.at[h, j], q_recv.at[h, j, 2]).wait()
            attend(h, j)
            send_out(h, j)
            return carry

        lax.fori_loop(0, RING, one, 0)
        return carry

    lax.fori_loop(0, PER, head, 0)

    for n, d in enumerate(steps):
        if d == 0:
            @pl.when(jnp.logical_not(home))
            def _():
                pltpu.make_async_copy(mine, mine, m_send.at[n]).wait()
        else:
            pltpu.make_async_copy(mine, mine, m_send.at[n]).wait()

    def inputs_left(h, carry):
        for n, d in enumerate(steps):
            for t in range(3):
                piece = qbuf.at[h, n]
                if d == 0:
                    @pl.when(jnp.logical_not(home))
                    def _():
                        pltpu.make_async_copy(piece, piece, q_send.at[h, n, t]).wait()
                else:
                    pltpu.make_async_copy(piece, piece, q_send.at[h, n, t]).wait()
        for side in range(2):
            edge_copy(h, side).wait_send()
        for place in range(6):
            for copy in forward_copies(h, place):
                copy.wait_send()
        return carry

    lax.fori_loop(0, PER, inputs_left, 0)

    def outputs_left(h, carry):
        for j in range(RING):
            place, parity = j // 2, j % 2

            @pl.when(jnp.logical_not(home & (place == hi) & (parity == core)))
            def _():
                piece = obuf.at[h, j]
                pltpu.make_async_copy(piece, piece, o_send.at[h, j]).wait()
        for s in range(RING):
            cols = pl.ds(pl.multiple_of((s * PER + h) * SIZE, SIZE), SIZE)
            piece = out_ref.at[:, cols]
            pltpu.make_async_copy(piece, piece, o_recv.at[h, s]).wait()
        return carry

    lax.fori_loop(0, PER, outputs_left, 0)


def shards(queries, keys, values, frame_mask, query_order):
    anywhere = pl.BlockSpec(memory_space=pl.ANY)
    dma = pltpu.SemaphoreType.DMA
    return pl.pallas_call(
        body,
        out_shape=pltpu.VMEM(queries.shape, queries.dtype),
        in_specs=[
            pl.BlockSpec(memory_space=pltpu.SMEM),
            pl.BlockSpec(memory_space=pltpu.VMEM),
            anywhere, anywhere, anywhere,
        ],
        out_specs=anywhere,
        scratch_shapes=[
            pltpu.VMEM((PER, RING, TOK, SIZE), jnp.bfloat16),
            pltpu.VMEM((PER, 6, 6, 2, TOK, SIZE), jnp.bfloat16),
            pltpu.VMEM((PER, RING, TOK, SIZE), jnp.bfloat16),
            pltpu.VMEM((2, SIZE), jnp.float32),
            pltpu.VMEM((RING, 2, SIZE), jnp.float32),
            pltpu.VMEM((RING, 30, 2, SIZE), jnp.float32),
            pltpu.VMEM((30, TOK, SIZE), jnp.float32),
            dma((PER, RING, 3)), dma((PER, RING, 3)),
            dma((PER, 2)), dma((PER, 2)),
            dma((PER, 6, 2)), dma((PER, 6, 2)),
            dma((RING,)), dma((RING,)),
            dma((PER, RING)), dma((PER, RING)),
        ],
        compiler_params=pltpu.CompilerParams(
            collective_id=0, has_side_effects=True, vmem_limit_bytes=62 << 20
        ),
        cost_estimate=pl.CostEstimate(
            flops=12_000_000_000, bytes_accessed=7_000_000, transcendentals=24_000_000
        ),
        name="ring_attention",
    )(query_order, frame_mask, queries, keys, values)


def solution(mesh):
    placed = (
        P(("inner", "outer"), None),
        P(("inner", "outer"), None),
        P(("inner", "outer"), None),
        P(("inner", "outer"), None),
        P(("inner", "outer")),
    )
    return jax.shard_map(
        shards, mesh=mesh, in_specs=placed, out_specs=P(("inner", "outer"), None), check_vma=False
    )
```

```python
import math

import jax
import jax.numpy as jnp
from jax import lax
from jax.experimental import pallas as pl
from jax.experimental.pallas import tpu as pltpu
from jax.sharding import PartitionSpec as P

HEADS = 24
SIZE = 128
RING = 8
PER = HEADS // RING
TOK = 256
MESH = pl.DeviceIdType.MESH
DEAD = -1e30
EXPONENT = math.log2(math.e) / math.sqrt(SIZE)


def body(order_ref, mask_ref, q_ref, k_ref, v_ref, out_ref,
         qbuf, kv, obuf, mine, marks, bias, score,
         q_send, q_recv, y_send, y_recv, f_send, f_recv, m_send, m_recv, o_send, o_recv):
    inner = lax.axis_index("inner")
    outer = lax.axis_index("outer")
    x, lo, core = inner // 4, (inner // 2) % 2, inner % 2
    y, hi = outer // 4, outer % 4
    z = 2 * hi + lo
    home = lo == core

    def device(x_at, y_at, z_at, core_at):
        return (x_at * 4 + (z_at % 2) * 2 + core_at, y_at * 4 + z_at // 2)

    def owner(place, parity):
        return device(x, y, 2 * place + core, parity)

    up = device(x, (y + 1) % 4, z, core)
    down = device(x, (y + 3) % 4, z, core)
    after = device((x + core) % 4, y, z, 1 - core)
    before = device((x + 3 + core) % 4, y, z, 1 - core)

    barrier = pltpu.get_barrier_semaphore()
    for d in range(1, RING):
        pl.semaphore_signal(
            barrier, inc=1, device_id=device(x, y, (z + d) % RING, lo), device_id_type=MESH
        )

    @pl.when(jnp.logical_not(home))
    def _():
        pl.semaphore_signal(barrier, inc=1, device_id=device(x, y, z, lo), device_id_type=MESH)

    for place in range(4):
        pl.semaphore_signal(
            barrier, inc=1, device_id=owner(place, 1 - lo), device_id_type=MESH
        )
    for peer in (up, down, device((x + 2 * core + 3) % 4, y, z, 1 - core)):
        pl.semaphore_signal(barrier, inc=1, device_id=peer, device_id_type=MESH)

    mine[...] = jnp.zeros_like(mine)
    for row in range(2):
        picked = order_ref[row] - 2 * (inner * 16 + outer)
        live = jnp.where(picked == 0, mask_ref[0:1, :], mask_ref[1:2, :])
        mine[row : row + 1, 0:30] = jnp.where(live > 0, 0.0, DEAD)

    pl.semaphore_wait(barrier, 15 - home.astype(jnp.int32))

    slot = 2 * hi + core

    def move(source, target, send, recv, to, local):
        if local is None:
            pltpu.make_async_remote_copy(
                src_ref=source, dst_ref=target, send_sem=send, recv_sem=recv,
                device_id=to, device_id_type=MESH,
            ).start()
        else:
            @pl.when(local)
            def _():
                pltpu.make_async_copy(source, target, recv).start()

            @pl.when(jnp.logical_not(local))
            def _():
                pltpu.make_async_remote_copy(
                    src_ref=source, dst_ref=target, send_sem=send, recv_sem=recv,
                    device_id=to, device_id_type=MESH,
                ).start()

    steps = (4, 3, 5, 2, 6, 1, 7, 0)
    def spread(h, t):
        for n, d in enumerate(steps):
            there = (z + d) % RING
            to = device(x, y, there, lo)
            cols = pl.ds(pl.multiple_of((there * PER + h) * SIZE, SIZE), SIZE)
            source = (k_ref, v_ref, q_ref)[t].at[:, cols]
            if t < 2:
                target = kv.at[h, 1 + hi, 2 + core, t]
            else:
                target = qbuf.at[h, slot]
            move(source, target, q_send.at[h, n, t], q_recv.at[h, slot, t], to,
                 home if d == 0 else None)

    def spread_kv(h, carry):
        spread(h, 0)
        spread(h, 1)
        return carry

    def spread_q(h, carry):
        spread(h, 2)
        return carry

    lax.fori_loop(0, PER, spread_kv, 0)
    for n, d in enumerate(steps):
        to = device(x, y, (z + d) % RING, lo)
        move(mine, marks.at[slot], m_send.at[n], m_recv.at[slot], to, home if d == 0 else None)
    lax.fori_loop(0, PER, spread_q, 0)

    def forward_copies(h, place):
        source = kv.at[h, place, pl.ds(2, 2)]
        return (
            pltpu.make_async_remote_copy(
                src_ref=source, dst_ref=kv.at[h, place, pl.ds(0, 2)],
                send_sem=f_send.at[h, place, 0], recv_sem=f_recv.at[h, place, 0],
                device_id=after, device_id_type=MESH),
            pltpu.make_async_remote_copy(
                src_ref=source, dst_ref=kv.at[h, place, pl.ds(4, 2)],
                send_sem=f_send.at[h, place, 1], recv_sem=f_recv.at[h, place, 1],
                device_id=before, device_id_type=MESH),
        )

    def edge_copy(h, side):
        return pltpu.make_async_remote_copy(
            src_ref=kv.at[h, 4 if side == 0 else 1, pl.ds(2, 2)],
            dst_ref=kv.at[h, 0 if side == 0 else 5, pl.ds(2, 2)],
            send_sem=y_send.at[h, side], recv_sem=y_recv.at[h, side],
            device_id=up if side == 0 else down, device_id_type=MESH)

    def send_out(h, j):
        place, parity = j // 2, j % 2
        cols = pl.ds(pl.multiple_of((z * PER + h) * SIZE, SIZE), SIZE)
        move(obuf.at[h, j], out_ref.at[:, cols], o_send.at[h, j], o_recv.at[h, z],
             owner(place, parity), home & (place == hi) & (parity == core))

    def attend(h, j):
        place, parity = j // 2, j % 2
        query = qbuf[h, j]
        top = jnp.full((TOK, SIZE), DEAD, jnp.float32)
        for s in range(15):
            step, side = s // 3, s % 3
            keyset = kv[h, place + side, parity + step, 0]
            raw = lax.dot_general(query, keyset, (((1,), (1,)), ((), ())),
                                  preferred_element_type=jnp.float32)
            for slot_at in range(2):
                w = 6 * step + 2 * side + slot_at
                part = raw[:, slot_at * SIZE : (slot_at + 1) * SIZE]
                upper = part[:SIZE] + bias[j, w, 0:1, :]
                lower = part[SIZE:] + bias[j, w, 1:2, :]
                part = jnp.concatenate([upper, lower], axis=0)
                score[2 * s + slot_at] = part
                top = jnp.maximum(top, part)
        top = jnp.max(top, axis=1, keepdims=True)
        total = jnp.zeros((TOK, SIZE), jnp.float32)
        numer = jnp.zeros((TOK, SIZE), jnp.float32)
        for s in range(15):
            step, side = s // 3, s % 3
            valset = kv[h, place + side, parity + step, 1]
            left = jnp.exp2((score[2 * s] - top) * EXPONENT)
            right = jnp.exp2((score[2 * s + 1] - top) * EXPONENT)
            total = total + left + right
            prob = jnp.concatenate([left, right], axis=1).astype(jnp.bfloat16)
            numer = numer + jnp.dot(prob, valset, preferred_element_type=jnp.float32)
        total = jnp.sum(total, axis=1, keepdims=True)
        obuf[h, j] = (numer / total).astype(jnp.bfloat16)

    def gather(h, carry):
        for n in range(4):
            place = (3, 0, 1, 2)[n]
            for parity in range(2):
                for t in range(2):
                    piece = kv.at[h, 1 + place, 2 + parity, t]
                    pltpu.make_async_copy(piece, piece, q_recv.at[h, 2 * place + parity, t]).wait()
            if place == 3:
                edge_copy(h, 0).start()
            if place == 0:
                edge_copy(h, 1).start()
            for copy in forward_copies(h, 1 + place):
                copy.start()
        for side in range(2):
            edge_copy(h, side).wait_recv()
            for copy in forward_copies(h, 5 * side):
                copy.start()
        return carry

    lax.fori_loop(0, PER, gather, 0)

    for s in range(RING):
        pltpu.make_async_copy(mine, marks.at[s], m_recv.at[s]).wait()

    def widen(s, carry):
        rows = marks[s]
        for w in range(30):
            bias[s, w] = jnp.broadcast_to(rows[:, w : w + 1], (2, SIZE))
        return carry

    lax.fori_loop(0, RING, widen, 0)

    def head(h, carry):
        for place in range(6):
            for copy in forward_copies(h, place):
                copy.wait_recv()

        def one(n, carry):
            rank = n // 2
            even = jnp.where(rank == 0, 4, jnp.where(rank == 1, 2, jnp.where(rank == 2, 6, 0)))
            odd = jnp.where(rank == 0, 3, jnp.where(rank == 1, 5, jnp.where(rank == 2, 1, 7)))
            away = jnp.where(home, even, odd)
            ranked = ((z - away + RING) % RING) // 2
            place = jnp.where(h == PER - 1, rank, ranked)
            flip = jnp.where(rank == 1, 0, 1)
            j = 2 * place + (n + flip) % 2
            pltpu.make_async_copy(qbuf.at[h, j], qbuf.at[h, j], q_recv.at[h, j, 2]).wait()
            attend(h, j)
            send_out(h, j)
            return carry

        lax.fori_loop(0, RING, one, 0)
        return carry

    lax.fori_loop(0, PER, head, 0)

    for n, d in enumerate(steps):
        if d == 0:
            @pl.when(jnp.logical_not(home))
            def _():
                pltpu.make_async_copy(mine, mine, m_send.at[n]).wait()
        else:
            pltpu.make_async_copy(mine, mine, m_send.at[n]).wait()

    def inputs_left(h, carry):
        for n, d in enumerate(steps):
            for t in range(3):
                piece = qbuf.at[h, n]
                if d == 0:
                    @pl.when(jnp.logical_not(home))
                    def _():
                        pltpu.make_async_copy(piece, piece, q_send.at[h, n, t]).wait()
                else:
                    pltpu.make_async_copy(piece, piece, q_send.at[h, n, t]).wait()
        for side in range(2):
            edge_copy(h, side).wait_send()
        for place in range(6):
            for copy in forward_copies(h, place):
                copy.wait_send()
        return carry

    lax.fori_loop(0, PER, inputs_left, 0)

    def outputs_left(h, carry):
        for j in range(RING):
            place, parity = j // 2, j % 2

            @pl.when(jnp.logical_not(home & (place == hi) & (parity == core)))
            def _():
                piece = obuf.at[h, j]
                pltpu.make_async_copy(piece, piece, o_send.at[h, j]).wait()
        for s in range(RING):
            cols = pl.ds(pl.multiple_of((s * PER + h) * SIZE, SIZE), SIZE)
            piece = out_ref.at[:, cols]
            pltpu.make_async_copy(piece, piece, o_recv.at[h, s]).wait()
        return carry

    lax.fori_loop(0, PER, outputs_left, 0)


def shards(queries, keys, values, frame_mask, query_order):
    anywhere = pl.BlockSpec(memory_space=pl.ANY)
    dma = pltpu.SemaphoreType.DMA
    return pl.pallas_call(
        body,
        out_shape=pltpu.VMEM(queries.shape, queries.dtype),
        in_specs=[
            pl.BlockSpec(memory_space=pltpu.SMEM),
            pl.BlockSpec(memory_space=pltpu.VMEM),
            anywhere, anywhere, anywhere,
        ],
        out_specs=anywhere,
        scratch_shapes=[
            pltpu.VMEM((PER, RING, TOK, SIZE), jnp.bfloat16),
            pltpu.VMEM((PER, 6, 6, 2, TOK, SIZE), jnp.bfloat16),
            pltpu.VMEM((PER, RING, TOK, SIZE), jnp.bfloat16),
            pltpu.VMEM((2, SIZE), jnp.float32),
            pltpu.VMEM((RING, 2, SIZE), jnp.float32),
            pltpu.VMEM((RING, 30, 2, SIZE), jnp.float32),
            pltpu.VMEM((30, TOK, SIZE), jnp.float32),
            dma((PER, RING, 3)), dma((PER, RING, 3)),
            dma((PER, 2)), dma((PER, 2)),
            dma((PER, 6, 2)), dma((PER, 6, 2)),
            dma((RING,)), dma((RING,)),
            dma((PER, RING)), dma((PER, RING)),
        ],
        compiler_params=pltpu.CompilerParams(
            collective_id=0, has_side_effects=True, vmem_limit_bytes=62 << 20
        ),
        cost_estimate=pl.CostEstimate(
            flops=12_000_000_000, bytes_accessed=7_000_000, transcendentals=24_000_000
        ),
        name="ring_attention",
    )(query_order, frame_mask, queries, keys, values)


def solution(mesh):
    placed = (
        P(("inner", "outer"), None),
        P(("inner", "outer"), None),
        P(("inner", "outer"), None),
        P(("inner", "outer"), None),
        P(("inner", "outer")),
    )
    return jax.shard_map(
        shards, mesh=mesh, in_specs=placed, out_specs=P(("inner", "outer"), None), check_vma=False
    )
```

```python
import math

import jax
import jax.numpy as jnp
from jax import lax
from jax.experimental import pallas as pl
from jax.experimental.pallas import tpu as pltpu
from jax.sharding import PartitionSpec as P

HEADS = 24
SIZE = 128
RING = 8
PER = HEADS // RING
TOK = 256
MESH = pl.DeviceIdType.MESH
DEAD = -1e30
EXPONENT = math.log2(math.e) / math.sqrt(SIZE)


def body(order_ref, mask_ref, q_ref, k_ref, v_ref, out_ref,
         qbuf, kv, obuf, mine, marks, bias, score,
         i_send, kv_recv, q_recv, y_send, y_recv, f_send, f_recv, m_send, m_recv, o_send, o_recv):
    inner = lax.axis_index("inner")
    outer = lax.axis_index("outer")
    x, lo, core = inner // 4, (inner // 2) % 2, inner % 2
    y, hi = outer // 4, outer % 4
    z = 2 * hi + lo
    home = lo == core

    def device(x_at, y_at, z_at, core_at):
        return (x_at * 4 + (z_at % 2) * 2 + core_at, y_at * 4 + z_at // 2)

    def owner(place, parity):
        return device(x, y, 2 * place + core, parity)

    up = device(x, (y + 1) % 4, z, core)
    down = device(x, (y + 3) % 4, z, core)
    after = device((x + core) % 4, y, z, 1 - core)
    before = device((x + 3 + core) % 4, y, z, 1 - core)

    barrier = pltpu.get_barrier_semaphore()
    for d in range(1, RING):
        pl.semaphore_signal(
            barrier, inc=1, device_id=device(x, y, (z + d) % RING, lo), device_id_type=MESH
        )

    @pl.when(jnp.logical_not(home))
    def _():
        pl.semaphore_signal(barrier, inc=1, device_id=device(x, y, z, lo), device_id_type=MESH)

    for place in range(4):
        pl.semaphore_signal(
            barrier, inc=1, device_id=owner(place, 1 - lo), device_id_type=MESH
        )
    for peer in (up, down, device((x + 2 * core + 3) % 4, y, z, 1 - core)):
        pl.semaphore_signal(barrier, inc=1, device_id=peer, device_id_type=MESH)

    mine[...] = jnp.zeros_like(mine)
    for row in range(2):
        picked = order_ref[row] - 2 * (inner * 16 + outer)
        live = jnp.where(picked == 0, mask_ref[0:1, :], mask_ref[1:2, :])
        mine[row : row + 1, 0:30] = jnp.where(live > 0, 0.0, DEAD)

    pl.semaphore_wait(barrier, 15 - home.astype(jnp.int32))

    slot = 2 * hi + core

    def move(source, target, send, recv, to, local):
        if local is None:
            pltpu.make_async_remote_copy(
                src_ref=source, dst_ref=target, send_sem=send, recv_sem=recv,
                device_id=to, device_id_type=MESH,
            ).start()
        else:
            @pl.when(local)
            def _():
                pltpu.make_async_copy(source, target, recv).start()

            @pl.when(jnp.logical_not(local))
            def _():
                pltpu.make_async_remote_copy(
                    src_ref=source, dst_ref=target, send_sem=send, recv_sem=recv,
                    device_id=to, device_id_type=MESH,
                ).start()

    steps = (4, 3, 5, 2, 6, 1, 7, 0)
    def spread(h, t):
        for d in steps:
            there = (z + d) % RING
            to = device(x, y, there, lo)
            cols = pl.ds(pl.multiple_of((there * PER + h) * SIZE, SIZE), SIZE)
            source = (k_ref, v_ref, q_ref)[t].at[:, cols]
            if t < 2:
                target = kv.at[h, 1 + hi, 2 + core, t]
            else:
                target = qbuf.at[h, slot]
            arrived = kv_recv.at[h] if t < 2 else q_recv.at[h]
            move(source, target, i_send.at[t], arrived, to, home if d == 0 else None)

    def spread_kv(h, carry):
        spread(h, 0)
        spread(h, 1)
        return carry

    def spread_q(h, carry):
        spread(h, 2)
        return carry

    lax.fori_loop(0, PER, spread_kv, 0)
    for d in steps:
        to = device(x, y, (z + d) % RING, lo)
        move(mine, marks.at[slot], m_send, m_recv, to, home if d == 0 else None)
    lax.fori_loop(0, PER, spread_q, 0)

    def forward_copies(h, place):
        source = kv.at[h, place, pl.ds(2, 2)]
        return (
            pltpu.make_async_remote_copy(
                src_ref=source, dst_ref=kv.at[h, place, pl.ds(0, 2)],
                send_sem=f_send.at[h], recv_sem=f_recv.at[h, 0],
                device_id=after, device_id_type=MESH),
            pltpu.make_async_remote_copy(
                src_ref=source, dst_ref=kv.at[h, place, pl.ds(4, 2)],
                send_sem=f_send.at[h], recv_sem=f_recv.at[h, 1],
                device_id=before, device_id_type=MESH),
        )

    def edge_copy(h, side):
        return pltpu.make_async_remote_copy(
            src_ref=kv.at[h, 4 if side == 0 else 1, pl.ds(2, 2)],
            dst_ref=kv.at[h, 0 if side == 0 else 5, pl.ds(2, 2)],
            send_sem=y_send, recv_sem=y_recv.at[h, side],
            device_id=up if side == 0 else down, device_id_type=MESH)

    def send_out(h, j):
        place, parity = j // 2, j % 2
        cols = pl.ds(pl.multiple_of((z * PER + h) * SIZE, SIZE), SIZE)
        move(obuf.at[h, j], out_ref.at[:, cols], o_send, o_recv,
             owner(place, parity), home & (place == hi) & (parity == core))

    def attend(h, j):
        place, parity = j // 2, j % 2
        query = qbuf[h, j]
        top = jnp.full((TOK, SIZE), DEAD, jnp.float32)
        for s in range(15):
            step, side = s // 3, s % 3
            keyset = kv[h, place + side, parity + step, 0]
            raw = lax.dot_general(query, keyset, (((1,), (1,)), ((), ())),
                                  preferred_element_type=jnp.float32)
            for slot_at in range(2):
                w = 6 * step + 2 * side + slot_at
                part = raw[:, slot_at * SIZE : (slot_at + 1) * SIZE]
                upper = part[:SIZE] + bias[j, w, 0:1, :]
                lower = part[SIZE:] + bias[j, w, 1:2, :]
                part = jnp.concatenate([upper, lower], axis=0)
                score[2 * s + slot_at] = part
                top = jnp.maximum(top, part)
        top = jnp.max(top, axis=1, keepdims=True)
        total = jnp.zeros((TOK, SIZE), jnp.float32)
        numer = jnp.zeros((TOK, SIZE), jnp.float32)
        for s in range(15):
            step, side = s // 3, s % 3
            valset = kv[h, place + side, parity + step, 1]
            left = jnp.exp2((score[2 * s] - top) * EXPONENT)
            right = jnp.exp2((score[2 * s + 1] - top) * EXPONENT)
            total = total + left + right
            prob = jnp.concatenate([left, right], axis=1).astype(jnp.bfloat16)
            numer = numer + jnp.dot(prob, valset, preferred_element_type=jnp.float32)
        total = jnp.sum(total, axis=1, keepdims=True)
        obuf[h, j] = (numer / total).astype(jnp.bfloat16)

    def settle(piece, sem):
        pltpu.make_async_copy(piece, piece, sem).wait()

    def gather(h, carry):
        settle(kv.at[h, pl.ds(1, 4), pl.ds(2, 2)], kv_recv.at[h])
        for side in range(2):
            edge_copy(h, side).start()
        for place in range(1, 5):
            for copy in forward_copies(h, place):
                copy.start()
        for side in range(2):
            edge_copy(h, side).wait_recv()
            for copy in forward_copies(h, 5 * side):
                copy.start()
        return carry

    lax.fori_loop(0, PER, gather, 0)

    settle(marks, m_recv)

    def widen(s, carry):
        rows = marks[s]
        for w in range(30):
            bias[s, w] = jnp.broadcast_to(rows[:, w : w + 1], (2, SIZE))
        return carry

    lax.fori_loop(0, RING, widen, 0)

    def head(h, carry):
        for side in range(2):
            settle(kv.at[h, :, pl.ds(4 * side, 2)], f_recv.at[h, side])
        settle(qbuf.at[h], q_recv.at[h])

        def one(n, carry):
            rank = n // 2
            even = jnp.where(rank == 0, 4, jnp.where(rank == 1, 2, jnp.where(rank == 2, 6, 0)))
            odd = jnp.where(rank == 0, 3, jnp.where(rank == 1, 5, jnp.where(rank == 2, 1, 7)))
            away = jnp.where(home, even, odd)
            ranked = ((z - away + RING) % RING) // 2
            place = jnp.where(h == PER - 1, rank, ranked)
            flip = jnp.where(rank == 1, 0, 1)
            j = 2 * place + (n + flip) % 2
            attend(h, j)
            send_out(h, j)
            return carry

        lax.fori_loop(0, RING, one, 0)
        return carry

    lax.fori_loop(0, PER, head, 0)

    def settle_sent(buffer, few, sem):
        @pl.when(home)
        def _():
            settle(few, sem)

        @pl.when(jnp.logical_not(home))
        def _():
            settle(buffer, sem)

    settle_sent(marks, marks.at[pl.ds(0, RING - 1)], m_send)
    for t in range(3):
        settle_sent(qbuf, qbuf.at[:, pl.ds(0, RING - 1)], i_send.at[t])
    settle(qbuf, y_send)
    for h in range(PER):
        settle(kv.at[h, :, pl.ds(0, 4)], f_send.at[h])
    settle_sent(obuf, obuf.at[:, pl.ds(0, RING - 1)], o_send)
    settle(out_ref, o_recv)


def shards(queries, keys, values, frame_mask, query_order):
    anywhere = pl.BlockSpec(memory_space=pl.ANY)
    dma = pltpu.SemaphoreType.DMA
    return pl.pallas_call(
        body,
        out_shape=pltpu.VMEM(queries.shape, queries.dtype),
        in_specs=[
            pl.BlockSpec(memory_space=pltpu.SMEM),
            pl.BlockSpec(memory_space=pltpu.VMEM),
            anywhere, anywhere, anywhere,
        ],
        out_specs=anywhere,
        scratch_shapes=[
            pltpu.VMEM((PER, RING, TOK, SIZE), jnp.bfloat16),
            pltpu.VMEM((PER, 6, 6, 2, TOK, SIZE), jnp.bfloat16),
            pltpu.VMEM((PER, RING, TOK, SIZE), jnp.bfloat16),
            pltpu.VMEM((2, SIZE), jnp.float32),
            pltpu.VMEM((RING, 2, SIZE), jnp.float32),
            pltpu.VMEM((RING, 30, 2, SIZE), jnp.float32),
            pltpu.VMEM((30, TOK, SIZE), jnp.float32),
            dma((3,)), dma((PER,)), dma((PER,)),
            dma, dma((PER, 2)),
            dma((PER,)), dma((PER, 2)),
            dma, dma,
            dma, dma,
        ],
        compiler_params=pltpu.CompilerParams(
            collective_id=0, has_side_effects=True, vmem_limit_bytes=62 << 20
        ),
        cost_estimate=pl.CostEstimate(
            flops=12_000_000_000, bytes_accessed=7_000_000, transcendentals=24_000_000
        ),
        name="ring_attention",
    )(query_order, frame_mask, queries, keys, values)


def solution(mesh):
    placed = (
        P(("inner", "outer"), None),
        P(("inner", "outer"), None),
        P(("inner", "outer"), None),
        P(("inner", "outer"), None),
        P(("inner", "outer")),
    )
    return jax.shard_map(
        shards, mesh=mesh, in_specs=placed, out_specs=P(("inner", "outer"), None), check_vma=False
    )
```
